32 devices in a mesh: groups: 2 (over x), patch: 16 (over z, y, core).
Axes of the slice: x: 2, y: 2, z: 4, core: 2. Of those that a mesh axis runs over, the one named last changes fastest.
Arguments:
- fine_latents: bfloat16 [20480, 512], P(('groups', 'patch')), parts along dimension 0, may hold values from -6 to 6
- coarse_latents: bfloat16 [5120, 512], P(('groups', 'patch')), parts along dimension 0, may hold values from -6 to 6
- up_weight: bfloat16 [512, 512], replicated, may hold values from -0.25 to 0.25
- down_weight: bfloat16 [512, 512], replicated, may hold values from -0.25 to 0.25
- fine_cotangent: bfloat16 [20480, 512], P(('groups', 'patch')), parts along dimension 0, may hold values from -6 to 6
- coarse_cotangent: bfloat16 [5120, 512], P(('groups', 'patch')), parts along dimension 0, may hold values from -6 to 6
- edge_fine: int32 [2, 24576], P(None, 'patch'), may hold values from 0 to 10239, as said below
- edge_coarse: int32 [2, 24576], P(None, 'patch'), may hold values from 0 to 2559, as said below
- block_counts: int32 [2, 384], P(None, 'patch'), may hold values from 16 to 64, as said below
Outputs:
- fine_grad: bfloat16 [20480, 512], P(('groups', 'patch')), parts along dimension 0
- coarse_grad: float32 [5120, 512], P(('groups', 'patch')), parts along dimension 0
- up_weight_grad: float32 [1024, 512], P(('groups', 'patch')), parts along dimension 0
- down_weight_grad: float32 [1024, 512], P(('groups', 'patch')), parts along dimension 0
The draws below stay inside these ranges and needn't reach their ends.
There are 2 independent parts, one for each index of `groups`. The reference program is written for one: setup_inputs(seed, part) draws one part's arguments, and reference() takes and returns one part's arrays. A program takes and returns all parts, laid end to end along the dimension named above; an argument that names none is the same for every part. Nothing has to cross between parts.
Inputs may be any that keep to these rules, and one draw needn't show every extreme that they name: Edge row r, in either direction, belongs to patch r // 1536, and its fine node is one of that patch's nodes (edge_fine // 640 equals the patch). Within one patch's 1536 rows of a direction, the first 1024 rows name coarse nodes of the same patch (edge_coarse // 160), the next 256 rows those of the patch one lower, the last 256 rows those of the patch one higher, cyclically. `block_counts`: each patch has a full block in each direction.
All inputs are finite; a program needn't handle non-finite values.
Results may differ from the reference program's by a relative error of at most 0.01.
Values may be sent and summed in bfloat16 or wider, within the bound.
A program may use at most 64 MiB of HBM per device.

```python
import math
import jax
import jax.numpy as jnp
from jax import lax

D = 512
CF = 640
CC = 160
BLOCK = 64
NB_OWN = 16
NB_SIDE = 4
BLOCKS_DEV = 24
EDGES_DEV = 1536
EDGES = 24576
BLOCKS = 384
NF = 10240
NC = 2560
N_PATCH = 16


def draw_edge_fine(key, part):
    key = jax.random.fold_in(key, 11)
    positions = jnp.arange(EDGES, dtype=jnp.int32)
    owners = positions // EDGES_DEV
    offsets = jax.random.randint(key, (2, EDGES), 0, CF, dtype=jnp.int32)
    values = owners[None, :] * CF + offsets
    values = values.at[:, 0].set(0)
    values = values.at[:, EDGES - 1].set(NF - 1)
    return values


def draw_edge_coarse(key, part):
    key = jax.random.fold_in(key, 23)
    positions = jnp.arange(EDGES, dtype=jnp.int32)
    within = positions % EDGES_DEV
    side_step = jnp.where(within < NB_OWN * BLOCK, 0, jnp.where(within < (NB_OWN + NB_SIDE) * BLOCK, -1, 1))
    owners = (positions // EDGES_DEV + side_step + N_PATCH) % N_PATCH
    offsets = jax.random.randint(key, (2, EDGES), 0, CC, dtype=jnp.int32)
    values = owners[None, :] * CC + offsets
    values = values.at[:, 0].set(0)
    values = values.at[:, (N_PATCH - 1) * EDGES_DEV].set(NC - 1)
    return values


def draw_block_counts(key, part):
    key = jax.random.fold_in(key, 37)
    first_key, second_key = jax.random.split(key)
    counts = jax.random.randint(first_key, (2, BLOCKS), BLOCK // 4, BLOCK + 1, dtype=jnp.int32)
    full_at = jax.random.randint(second_key, (2, N_PATCH), 0, BLOCKS_DEV, dtype=jnp.int32)
    block_ids = jnp.arange(BLOCKS, dtype=jnp.int32)
    chosen = jnp.take(full_at, block_ids // BLOCKS_DEV, axis=1)
    return jnp.where((block_ids % BLOCKS_DEV)[None, :] == chosen, BLOCK, counts)


def with_spikes(result, rng, source, target, parts, factor):
    owner, partner = [(jnp.arange(result.shape[axis_at]) // (result.shape[axis_at] // parts)).reshape([-1 if axis == axis_at else 1 for axis in range(result.ndim)]) for axis_at in (source, target)]
    chosen = jax.random.permutation(rng, parts)[partner]
    strong = (owner == chosen) | (owner == (partner + parts // 2) % parts)
    return jnp.where(strong, factor * result, result)


def block_scale(rng, extent, cuts, least, high):
    loudness = 1.0
    for position, blocks in cuts:
        steps = jax.random.uniform(jax.random.fold_in(jax.random.fold_in(rng, 6), position), (blocks,), jnp.float32, least / len(cuts), high / len(cuts))
        loudness = loudness * jnp.repeat(jnp.exp(steps), extent[position] // blocks).reshape((-1,) + (1,) * (len(extent) - 1 - position))
    return loudness


def bell_draw(stream_key, extent, deviation, bound, shards=(), held_as=jnp.bfloat16):
    level = block_scale(stream_key, extent, shards, -0.22, 0.18) if shards else 1.0
    result = jax.random.normal(stream_key, extent, jnp.float32) * deviation * level
    return jnp.minimum(jnp.maximum(result, -bound), bound).astype(held_as)


def noise_with(stream_key, dims, spread, bound, cuts, heavy, held_as=jnp.bfloat16):
    entries = spread * jax.random.normal(stream_key, dims, jnp.float32)
    if cuts:
        entries = entries * block_scale(stream_key, dims, cuts, -0.22, 0.18)
    return jnp.clip(with_spikes(entries, jax.random.fold_in(stream_key, 3), *heavy), -bound, bound).astype(held_as)


def setup_inputs(seed: int = 0, part: int = 0) -> dict:
    key_of = jax.random.split(jax.random.key(seed), 10)
    own_keys = jax.random.split(jax.random.fold_in(key_of[9], part), 10)
    fine_latents = noise_with(own_keys[0], (NF, D), 1.0, 6.0, ((0, 16),), (0, 1, 16, 2.0))
    coarse_latents = noise_with(own_keys[1], (NC, D), 1.0, 6.0, ((0, 16),), (0, 1, 16, 2.0))
    up_weight = bell_draw(key_of[2], (D, D), D ** -0.5, 0.25)
    down_weight = bell_draw(key_of[3], (D, D), D ** -0.5, 0.25)
    fine_cotangent = bell_draw(own_keys[4], (NF, D), 1.0, 6.0, ((0, 16),))
    coarse_cotangent = bell_draw(own_keys[5], (NC, D), 1.0, 6.0, ((0, 16),))
    edge_fine = draw_edge_fine(jax.random.fold_in(key_of[9], 71), part)
    edge_coarse = draw_edge_coarse(jax.random.fold_in(key_of[9], 71), part)
    block_counts = draw_block_counts(jax.random.fold_in(key_of[9], 71), part)
    return dict(fine_latents=fine_latents, coarse_latents=coarse_latents, up_weight=up_weight, down_weight=down_weight, fine_cotangent=fine_cotangent, coarse_cotangent=coarse_cotangent, edge_fine=edge_fine, edge_coarse=edge_coarse, block_counts=block_counts)


def silu_slope(values):
    sigm = jax.nn.sigmoid(values)
    return sigm * (1.0 + values * (1.0 - sigm))

def per_patch(values):
    return values.reshape(N_PATCH, EDGES_DEV)

def reference(fine_latents, coarse_latents, up_weight, down_weight, fine_cotangent, coarse_cotangent, edge_fine, edge_coarse, block_counts):
    edge_index = jnp.arange(EDGES, dtype=jnp.int32)
    count_rows = jnp.take(block_counts, edge_index // BLOCK, axis=1)
    row_mask = ((edge_index % BLOCK)[None, :] < count_rows).astype(jnp.float32)
    grad_scale = 1.0 / math.sqrt(EDGES)

    def down_step(carried, inputs):
        coarse_acc, weight_acc = carried
        fine_idx, coarse_idx, edge_mask = inputs
        gathered = jnp.take(coarse_latents, coarse_idx, axis=0)
        pre_act = jnp.dot(gathered, down_weight, preferred_element_type=jnp.float32)
        incoming = jnp.take(fine_cotangent, fine_idx, axis=0).astype(jnp.float32) * edge_mask[:, None]
        delta_b = (incoming * silu_slope(pre_act)).astype(jnp.bfloat16)
        weight_acc = weight_acc + lax.dot_general(gathered, delta_b, (((0,), (0,)), ((), ())), preferred_element_type=jnp.float32)
        back_terms = lax.dot_general(delta_b, down_weight, (((1,), (1,)), ((), ())), preferred_element_type=jnp.float32)
        coarse_acc = coarse_acc + jax.ops.segment_sum(back_terms, coarse_idx, num_segments=NC)
        return ((coarse_acc, weight_acc), None)
    start_down = (jnp.zeros((NC, D), jnp.float32), jnp.zeros((D, D), jnp.float32))
    (coarse_sum, down_acc), unused = lax.scan(down_step, start_down, (per_patch(edge_fine[1]), per_patch(edge_coarse[1]), per_patch(row_mask[1])))
    coarse_grad = coarse_cotangent.astype(jnp.float32) + coarse_sum
    coarse_grad_b = coarse_grad.astype(jnp.bfloat16)

    def up_step(weight_acc, inputs):
        patch_id, fine_idx, coarse_idx, edge_mask = inputs
        gathered = jnp.take(fine_latents, fine_idx, axis=0)
        pre_act = jnp.dot(gathered, up_weight, preferred_element_type=jnp.float32)
        incoming = jnp.take(coarse_grad_b, coarse_idx, axis=0).astype(jnp.float32) * edge_mask[:, None]
        delta_b = (incoming * silu_slope(pre_act)).astype(jnp.bfloat16)
        weight_acc = weight_acc + lax.dot_general(gathered, delta_b, (((0,), (0,)), ((), ())), preferred_element_type=jnp.float32)
        back_terms = lax.dot_general(delta_b, up_weight, (((1,), (1,)), ((), ())), preferred_element_type=jnp.float32)
        local_terms = jax.ops.segment_sum(back_terms, fine_idx - patch_id * CF, num_segments=CF)
        return (weight_acc, local_terms)
    patch_ids = jnp.arange(N_PATCH, dtype=jnp.int32)
    up_acc, fine_terms = lax.scan(up_step, jnp.zeros((D, D), jnp.float32), (patch_ids, per_patch(edge_fine[0]), per_patch(edge_coarse[0]), per_patch(row_mask[0])))
    fine_grad = (fine_cotangent.astype(jnp.float32) + fine_terms.reshape(NF, D)).astype(jnp.bfloat16)
    return (fine_grad, coarse_grad, up_acc * grad_scale, down_acc * grad_scale)
```

```python
import functools
import math

import jax
import jax.numpy as jnp
from jax import lax
from jax.experimental import pallas as pl
from jax.experimental.pallas import tpu as pltpu
from jax.sharding import PartitionSpec as P

NB_OWN = 16
NB_SIDE = 4
MESH = pl.DeviceIdType.MESH
F32 = jnp.float32
BF16 = jnp.bfloat16
NN = (((1,), (0,)), ((), ()))
NT = (((1,), (1,)), ((), ()))
TN = (((0,), (0,)), ((), ()))


def mm(a, b, dims):
    return lax.dot_general(a, b, dims, preferred_element_type=F32)


def silu_slope(values):
    sigm = 1.0 / (1.0 + jnp.exp(-values))
    return sigm * (1.0 + values * (1.0 - sigm))


def one_hot(index, count):
    rows = lax.broadcasted_iota(jnp.int32, (count, index.shape[1]), 0)
    return jnp.where(rows == index, 1.0, 0.0).astype(BF16)


def kernel(
    n,
    fine_ref,
    coarse_ref,
    up_w,
    down_w,
    fine_cot,
    coarse_cot,
    edge_fine,
    edge_coarse,
    counts,
    fine_out,
    coarse_out,
    up_out,
    down_out,
    u_send,
    u_recv,
    g_own,
    g_recv,
    slope_f,
    fine_t,
    adj_up,
    terms,
    half_recv,
    half_sum,
    peer_recv,
    halo_send_sem,
    halo_recv_sem,
    half_send_sem,
    half_recv_sem,
    peer_send_sem,
    peer_recv_sem,
):
    me = lax.axis_index("patch")
    lower, upper = lax.rem(me + n - 1, n), lax.rem(me + 1, n)
    chips = n // 2
    chip, core = me // 2, lax.rem(me, 2)
    partner = chip * 2 + (1 - core)
    fine_count, width = fine_ref.shape
    coarse_count = coarse_ref.shape[0]
    edge_count = edge_fine.shape[1]
    blocks = counts.shape[1]
    block_len = edge_count // blocks
    own_rows, side_rows = NB_OWN * block_len, NB_SIDE * block_len
    chunk = width // n
    scale = 1.0 / math.sqrt(n * edge_count)
    wire = terms.dtype

    def peer(k):
        return lax.rem(chip + k, chips) * 2 + core

    barrier = pltpu.get_barrier_semaphore()
    for device in [lower, upper] + [peer(k) for k in range(1, chips)]:
        pl.semaphore_signal(barrier, inc=1, device_id={"patch": device}, device_id_type=MESH)

    spread = lax.broadcasted_iota(jnp.int32, (blocks, edge_count), 1) // block_len
    spread = spread == lax.broadcasted_iota(jnp.int32, (blocks, edge_count), 0)
    spread = jnp.where(spread, 1.0, 0.0).astype(BF16)
    count_rows = mm(counts[...].astype(F32).astype(BF16), spread, NN)
    position = lax.broadcasted_iota(jnp.int32, (1, edge_count), 1) % block_len
    regions = (
        (0, own_rows, me),
        (own_rows, side_rows, lower),
        (own_rows + side_rows, side_rows, upper),
    )

    def selectors(direction, region):
        start, size, owner = region
        lanes = slice(start, start + size)
        valid = position[:, lanes] < count_rows[direction : direction + 1, lanes].astype(jnp.int32)
        coarse = edge_coarse[direction : direction + 1, lanes] - owner * coarse_count
        coarse = jnp.where(valid, coarse, -1)
        fine = edge_fine[direction : direction + 1, lanes] - me * fine_count
        return one_hot(coarse, coarse_count), one_hot(fine, fine_count)

    def gathered_sum(region):
        coarse_sel, fine_sel = selectors(1, region)
        adjacency = mm(coarse_sel, fine_sel, NT).astype(BF16)
        return mm(adjacency, fine_cot[...], NN)

    def remote(src, dst, send_sem, recv_sem, device):
        return pltpu.make_async_remote_copy(
            src_ref=src,
            dst_ref=dst,
            send_sem=send_sem,
            recv_sem=recv_sem,
            device_id={"patch": device},
            device_id_type=MESH,
        )

    u_copies = [
        remote(
            u_send.at[s], u_recv.at[s], halo_send_sem.at[s], halo_recv_sem.at[s], (lower, upper)[s]
        )
        for s in range(2)
    ]
    u_send[0] = gathered_sum(regions[1]).astype(BF16)
    pl.semaphore_wait(barrier, chips + 1)
    u_copies[0].start()
    u_send[1] = gathered_sum(regions[2]).astype(BF16)
    u_copies[1].start()

    u_sum = gathered_sum(regions[0])
    slope_c = silu_slope(mm(coarse_ref[...], down_w[...], NN))
    for i, region in enumerate(regions):
        coarse_sel, fine_sel = selectors(0, region)
        adj_up[i] = mm(fine_sel, coarse_sel, NT).astype(BF16)
    slope_f[...] = silu_slope(mm(fine_ref[...], up_w[...], NN))
    fine_t[...] = fine_ref[...].T

    for copy in u_copies:
        copy.wait()
    u_sum = u_sum + u_recv[0].astype(F32) + u_recv[1].astype(F32)
    delta_c = (slope_c * u_sum).astype(BF16)
    coarse_grad = coarse_cot[...].astype(F32) + mm(delta_c, down_w[...], NT)
    coarse_out[...] = coarse_grad
    g_own[...] = coarse_grad.astype(BF16)
    g_copies = [
        remote(
            g_own, g_recv.at[s], halo_send_sem.at[2 + s], halo_recv_sem.at[2 + s], (lower, upper)[s]
        )
        for s in range(2)
    ]
    for copy in g_copies:
        copy.start()

    def half_copy(which):
        return remote(
            terms.at[which, 1 - core],
            half_recv.at[which],
            half_send_sem.at[which],
            half_recv_sem.at[which],
            partner,
        )

    def put_term(which, term):
        term = term.reshape(chips, 2, chunk, width)
        for parity in range(2):
            terms[which, parity] = term[:, parity].astype(wire)
        half_copy(which).start()

    def peer_copy(which, k):
        return remote(
            half_sum.at[which, lax.rem(chip + k, chips)],
            peer_recv.at[which, k - 1],
            peer_send_sem.at[which, k - 1],
            peer_recv_sem.at[which, k - 1],
            peer(k),
        )

    def send_peers(which):
        half_copy(which).wait()
        total = terms[which, core].astype(F32) + half_recv[which].astype(F32)
        half_sum[which] = total.astype(wire)
        for k in range(1, chips):
            peer_copy(which, k).start()

    def finish(which, out_ref):
        total = half_sum[which, chip].astype(F32)
        for k in range(1, chips):
            peer_copy(which, k).wait()
            total = total + peer_recv[which, k - 1].astype(F32)
        out_ref[...] = total * scale

    put_term(0, mm(coarse_ref[...], delta_c, TN))
    v_sum = mm(adj_up[0], g_own[...], NN)
    for copy in g_copies:
        copy.wait()
    send_peers(0)
    v_sum = v_sum + mm(adj_up[1], g_recv[1], NN) + mm(adj_up[2], g_recv[0], NN)
    delta_f = (slope_f[...] * v_sum).astype(BF16)
    put_term(1, mm(fine_t[...], delta_f, NN))
    fine_sum = mm(delta_f, up_w[...], NT)
    fine_out[...] = (fine_cot[...].astype(F32) + fine_sum).astype(BF16)
    send_peers(1)
    finish(0, down_out)
    finish(1, up_out)


def on_device(
    fine_latents,
    coarse_latents,
    up_weight,
    down_weight,
    fine_cotangent,
    coarse_cotangent,
    edge_fine,
    edge_coarse,
    block_counts,
):
    n = lax.axis_size("patch")
    fine_count, width = fine_latents.shape
    coarse_count = coarse_latents.shape[0]
    chunk, chips = width // n, n // 2
    wire = BF16 if chunk % 16 == 0 else F32
    vmem = pl.BlockSpec(memory_space=pltpu.VMEM)
    dma = pltpu.SemaphoreType.DMA
    return pl.pallas_call(
        functools.partial(kernel, n),
        out_shape=(
            jax.ShapeDtypeStruct((fine_count, width), BF16),
            jax.ShapeDtypeStruct((coarse_count, width), F32),
            jax.ShapeDtypeStruct((chunk, width), F32),
            jax.ShapeDtypeStruct((chunk, width), F32),
        ),
        in_specs=[vmem] * 9,
        out_specs=[vmem] * 4,
        scratch_shapes=[
            pltpu.VMEM((2, coarse_count, width), BF16),
            pltpu.VMEM((2, coarse_count, width), BF16),
            pltpu.VMEM((coarse_count, width), BF16),
            pltpu.VMEM((2, coarse_count, width), BF16),
            pltpu.VMEM((fine_count, width), F32),
            pltpu.VMEM((width, fine_count), BF16),
            pltpu.VMEM((3, fine_count, coarse_count), BF16),
            pltpu.VMEM((2, 2, chips, chunk, width), wire),
            pltpu.VMEM((2, chips, chunk, width), wire),
            pltpu.VMEM((2, chips, chunk, width), wire),
            pltpu.VMEM((2, chips - 1, chunk, width), wire),
            dma((4,)),
            dma((4,)),
            dma((2,)),
            dma((2,)),
            dma((2, chips - 1)),
            dma((2, chips - 1)),
        ],
        compiler_params=pltpu.CompilerParams(
            collective_id=0, has_side_effects=True, vmem_limit_bytes=48 * 2**20
        ),
        cost_estimate=pl.CostEstimate(
            flops=4 * 10**9, bytes_accessed=4 * 10**6, transcendentals=4 * 10**5
        ),
    )(
        fine_latents,
        coarse_latents,
        up_weight,
        down_weight,
        fine_cotangent,
        coarse_cotangent,
        edge_fine,
        edge_coarse,
        block_counts,
    )


def solution(mesh):
    nodes = P(("groups", "patch"), None)
    edges = P(None, "patch")
    return jax.shard_map(
        on_device,
        mesh=mesh,
        in_specs=(nodes, nodes, P(), P(), nodes, nodes, edges, edges, edges),
        out_specs=(nodes, nodes, nodes, nodes),
        check_vma=False,
    )
```

```python
import functools
import math

import jax
import jax.numpy as jnp
from jax import lax
from jax.experimental import pallas as pl
from jax.experimental.pallas import tpu as pltpu
from jax.sharding import PartitionSpec as P

NB_OWN = 16
NB_SIDE = 4
VMEM_LIMIT = 61 * 2**20
MESH = pl.DeviceIdType.MESH
F32 = jnp.float32
BF16 = jnp.bfloat16
NN = (((1,), (0,)), ((), ()))
NT = (((1,), (1,)), ((), ()))
TN = (((0,), (0,)), ((), ()))


def mm(a, b, dims):
    return lax.dot_general(a, b, dims, preferred_element_type=F32)


def silu_slope(values):
    sigm = 1.0 / (1.0 + jnp.exp(-values))
    return sigm * (1.0 + values * (1.0 - sigm))


def one_hot(index, count):
    rows = lax.broadcasted_iota(jnp.int32, (count, index.shape[1]), 0)
    return jnp.where(rows == index, 1.0, 0.0).astype(BF16)


def kernel(
    n,
    fine_hbm,
    coarse_hbm,
    up_w_hbm,
    down_w_hbm,
    fine_cot_hbm,
    coarse_cot_hbm,
    edge_fine_hbm,
    edge_coarse_hbm,
    counts_hbm,
    fine_hbm_out,
    coarse_hbm_out,
    up_hbm_out,
    down_hbm_out,
    fine_ref,
    coarse_ref,
    up_w,
    down_w,
    fine_cot,
    coarse_cot,
    edge_fine,
    edge_coarse,
    counts,
    load_sem,
    fine_out,
    coarse_out,
    up_out,
    down_out,
    store_sem,
    u_send,
    u_recv,
    g_own,
    g_recv,
    slope_f,
    fine_t,
    adj_up,
    terms,
    half_recv,
    half_sum,
    peer_recv,
    halo_send_sem,
    halo_recv_sem,
    half_send_sem,
    half_recv_sem,
    peer_send_sem,
    peer_recv_sem,
):
    me = lax.axis_index("patch")
    lower, upper = lax.rem(me + n - 1, n), lax.rem(me + 1, n)
    chips = n // 2
    chip, core = me // 2, lax.rem(me, 2)
    partner = chip * 2 + (1 - core)
    fine_count, width = fine_ref.shape
    coarse_count = coarse_ref.shape[0]
    edge_count = edge_fine.shape[1]
    blocks = counts.shape[1]
    block_len = edge_count // blocks
    own_rows, side_rows = NB_OWN * block_len, NB_SIDE * block_len
    chunk = width // n
    scale = 1.0 / math.sqrt(n * edge_count)
    wire = terms.dtype

    def peer(k):
        return lax.rem(chip + k, chips) * 2 + core

    loads = [
        pltpu.make_async_copy(src, dst, load_sem.at[i])
        for i, (src, dst) in enumerate(
            (
                (counts_hbm, counts),
                (edge_coarse_hbm, edge_coarse),
                (edge_fine_hbm, edge_fine),
                (fine_cot_hbm, fine_cot),
                (down_w_hbm, down_w),
                (coarse_hbm, coarse_ref),
                (coarse_cot_hbm, coarse_cot),
                (fine_hbm, fine_ref),
                (up_w_hbm, up_w),
            )
        )
    ]
    for copy in loads:
        copy.start()
    stores = [
        pltpu.make_async_copy(src, dst, store_sem.at[i])
        for i, (src, dst) in enumerate(
            (
                (fine_out, fine_hbm_out),
                (coarse_out, coarse_hbm_out),
                (up_out, up_hbm_out),
                (down_out, down_hbm_out),
            )
        )
    ]
    barrier = pltpu.get_barrier_semaphore()
    for device in [lower, upper] + [peer(k) for k in range(1, chips)]:
        pl.semaphore_signal(barrier, inc=1, device_id={"patch": device}, device_id_type=MESH)

    for copy in loads[:3]:
        copy.wait()
    spread = lax.broadcasted_iota(jnp.int32, (blocks, edge_count), 1) // block_len
    spread = spread == lax.broadcasted_iota(jnp.int32, (blocks, edge_count), 0)
    spread = jnp.where(spread, 1.0, 0.0).astype(BF16)
    count_rows = mm(counts[...].astype(F32).astype(BF16), spread, NN)
    position = lax.broadcasted_iota(jnp.int32, (1, edge_count), 1) % block_len
    regions = (
        (0, own_rows, me),
        (own_rows, side_rows, lower),
        (own_rows + side_rows, side_rows, upper),
    )

    def selectors(direction, region):
        start, size, owner = region
        lanes = slice(start, start + size)
        valid = position[:, lanes] < count_rows[direction : direction + 1, lanes].astype(jnp.int32)
        coarse = edge_coarse[direction : direction + 1, lanes] - owner * coarse_count
        coarse = jnp.where(valid, coarse, -1)
        fine = edge_fine[direction : direction + 1, lanes] - me * fine_count
        return one_hot(coarse, coarse_count), one_hot(fine, fine_count)

    def down_adjacency(region):
        coarse_sel, fine_sel = selectors(1, region)
        return mm(coarse_sel, fine_sel, NT).astype(BF16)

    def remote(src, dst, send_sem, recv_sem, device):
        return pltpu.make_async_remote_copy(
            src_ref=src,
            dst_ref=dst,
            send_sem=send_sem,
            recv_sem=recv_sem,
            device_id={"patch": device},
            device_id_type=MESH,
        )

    u_copies = [
        remote(
            u_send.at[s], u_recv.at[s], halo_send_sem.at[s], halo_recv_sem.at[s], (lower, upper)[s]
        )
        for s in range(2)
    ]
    adj_lower, adj_upper = down_adjacency(regions[1]), down_adjacency(regions[2])
    loads[3].wait()
    u_send[0] = mm(adj_lower, fine_cot[...], NN).astype(BF16)
    pl.semaphore_wait(barrier, chips + 1)
    u_copies[0].start()
    u_send[1] = mm(adj_upper, fine_cot[...], NN).astype(BF16)
    u_copies[1].start()

    u_sum = mm(down_adjacency(regions[0]), fine_cot[...], NN)
    for copy in loads[4:]:
        copy.wait()
    slope_c = silu_slope(mm(coarse_ref[...], down_w[...], NN))
    fine_t[...] = fine_ref[...].T
    slope_f[...] = silu_slope(mm(fine_ref[...], up_w[...], NN))

    for copy in u_copies:
        copy.wait()
    u_sum = u_sum + u_recv[0].astype(F32) + u_recv[1].astype(F32)
    delta_c = (slope_c * u_sum).astype(BF16)
    coarse_grad = coarse_cot[...].astype(F32) + mm(delta_c, down_w[...], NT)
    coarse_out[...] = coarse_grad
    g_own[...] = coarse_grad.astype(BF16)
    g_copies = [
        remote(
            g_own, g_recv.at[s], halo_send_sem.at[2 + s], halo_recv_sem.at[2 + s], (lower, upper)[s]
        )
        for s in range(2)
    ]
    for copy in g_copies:
        copy.start()
    stores[1].start()

    def half_copy(which):
        return remote(
            terms.at[which, 1 - core],
            half_recv.at[which],
            half_send_sem.at[which],
            half_recv_sem.at[which],
            partner,
        )

    def put_term(which, term):
        term = term.reshape(chips, 2, chunk, width)
        for parity in range(2):
            terms[which, parity] = term[:, parity].astype(wire)
        half_copy(which).start()

    def peer_copy(which, k):
        return remote(
            half_sum.at[which, lax.rem(chip + k, chips)],
            peer_recv.at[which, k - 1],
            peer_send_sem.at[which, k - 1],
            peer_recv_sem.at[which, k - 1],
            peer(k),
        )

    def send_peers(which):
        half_copy(which).wait()
        total = terms[which, core].astype(F32) + half_recv[which].astype(F32)
        half_sum[which] = total.astype(wire)
        for k in range(1, chips):
            peer_copy(which, k).start()

    def finish(which, out_ref):
        total = half_sum[which, chip].astype(F32)
        for k in range(1, chips):
            peer_copy(which, k).wait()
            total = total + peer_recv[which, k - 1].astype(F32)
        out_ref[...] = total * scale

    put_term(0, mm(coarse_ref[...], delta_c, TN))
    for i, region in enumerate(regions):
        coarse_sel, fine_sel = selectors(0, region)
        adj_up[i] = mm(fine_sel, coarse_sel, NT).astype(BF16)
    v_sum = mm(adj_up[0], g_own[...], NN)
    for copy in g_copies:
        copy.wait()
    send_peers(0)
    v_sum = v_sum + mm(adj_up[1], g_recv[1], NN) + mm(adj_up[2], g_recv[0], NN)
    delta_f = (slope_f[...] * v_sum).astype(BF16)
    put_term(1, mm(fine_t[...], delta_f, NN))
    fine_sum = mm(delta_f, up_w[...], NT)
    fine_out[...] = (fine_cot[...].astype(F32) + fine_sum).astype(BF16)
    stores[0].start()
    send_peers(1)
    finish(0, down_out)
    stores[3].start()
    finish(1, up_out)
    stores[2].start()
    for copy in stores:
        copy.wait()


def store_kernel(*refs):
    count = len(refs) // 2
    sems = refs[-1]
    copies = [
        pltpu.make_async_copy(refs[i], refs[count + i], sems.at[i]) for i in range(count)
    ]
    for copy in copies:
        copy.start()
    for copy in copies:
        copy.wait()


def on_device(
    fine_latents,
    coarse_latents,
    up_weight,
    down_weight,
    fine_cotangent,
    coarse_cotangent,
    edge_fine,
    edge_coarse,
    block_counts,
):
    n = lax.axis_size("patch")
    fine_count, width = fine_latents.shape
    coarse_count = coarse_latents.shape[0]
    chunk, chips = width // n, n // 2
    wire = BF16 if chunk % 16 == 0 else F32
    hbm = pl.BlockSpec(memory_space=pltpu.HBM)
    dma = pltpu.SemaphoreType.DMA
    arguments = (
        fine_latents,
        coarse_latents,
        up_weight,
        down_weight,
        fine_cotangent,
        coarse_cotangent,
        edge_fine,
        edge_coarse,
        block_counts,
    )
    out_shape = (
        jax.ShapeDtypeStruct((fine_count, width), BF16),
        jax.ShapeDtypeStruct((coarse_count, width), F32),
        jax.ShapeDtypeStruct((chunk, width), F32),
        jax.ShapeDtypeStruct((chunk, width), F32),
    )
    results = pl.pallas_call(
        functools.partial(kernel, n),
        out_shape=out_shape,
        in_specs=[hbm] * 9,
        out_specs=[hbm] * 4,
        scratch_shapes=[pltpu.VMEM(value.shape, value.dtype) for value in arguments]
        + [
            dma((9,)),
        ]
        + [pltpu.VMEM(value.shape, value.dtype) for value in out_shape]
        + [
            dma((4,)),
            pltpu.VMEM((2, coarse_count, width), BF16),
            pltpu.VMEM((2, coarse_count, width), BF16),
            pltpu.VMEM((coarse_count, width), BF16),
            pltpu.VMEM((2, coarse_count, width), BF16),
            pltpu.VMEM((fine_count, width), F32),
            pltpu.VMEM((width, fine_count), BF16),
            pltpu.VMEM((3, fine_count, coarse_count), BF16),
            pltpu.VMEM((2, 2, chips, chunk, width), wire),
            pltpu.VMEM((2, chips, chunk, width), wire),
            pltpu.VMEM((2, chips, chunk, width), wire),
            pltpu.VMEM((2, chips - 1, chunk, width), wire),
            dma((4,)),
            dma((4,)),
            dma((2,)),
            dma((2,)),
            dma((2, chips - 1)),
            dma((2, chips - 1)),
        ],
        compiler_params=pltpu.CompilerParams(
            collective_id=0, has_side_effects=True, vmem_limit_bytes=VMEM_LIMIT
        ),
        cost_estimate=pl.CostEstimate(
            flops=4 * 10**9, bytes_accessed=4 * 10**6, transcendentals=4 * 10**5
        ),
    )(*arguments)
    return pl.pallas_call(
        store_kernel,
        out_shape=out_shape,
        in_specs=[hbm] * 4,
        out_specs=[hbm] * 4,
        scratch_shapes=[dma((4,))],
        compiler_params=pltpu.CompilerParams(vmem_limit_bytes=VMEM_LIMIT),
    )(*results)


def solution(mesh):
    nodes = P(("groups", "patch"), None)
    edges = P(None, "patch")
    return jax.shard_map(
        on_device,
        mesh=mesh,
        in_specs=(nodes, nodes, P(), P(), nodes, nodes, edges, edges, edges),
        out_specs=(nodes, nodes, nodes, nodes),
        check_vma=False,
    )
```

```python
import functools
import math

import jax
import jax.numpy as jnp
from jax import lax
from jax.experimental import pallas as pl
from jax.experimental.pallas import tpu as pltpu
from jax.sharding import PartitionSpec as P

NB_OWN = 16
NB_SIDE = 4
VMEM_LIMIT = 61 * 2**20
MESH = pl.DeviceIdType.MESH
F32 = jnp.float32
BF16 = jnp.bfloat16
NN = (((1,), (0,)), ((), ()))
NT = (((1,), (1,)), ((), ()))
TN = (((0,), (0,)), ((), ()))


def mm(a, b, dims):
    return lax.dot_general(a, b, dims, preferred_element_type=F32)


def silu_slope(values):
    sigm = 1.0 / (1.0 + jnp.exp(-values))
    return sigm * (1.0 + values * (1.0 - sigm))


def one_hot(index, count):
    rows = lax.broadcasted_iota(jnp.int32, (count, index.shape[1]), 0)
    return jnp.where(rows == index, 1.0, 0.0).astype(BF16)


def kernel(
    n,
    fine_hbm,
    coarse_hbm,
    up_w_hbm,
    down_w_hbm,
    fine_cot_hbm,
    coarse_cot_hbm,
    edge_fine_hbm,
    edge_coarse_hbm,
    counts_hbm,
    fine_hbm_out,
    coarse_hbm_out,
    up_hbm_out,
    down_hbm_out,
    fine_ref,
    coarse_ref,
    up_w,
    down_w,
    fine_cot,
    coarse_cot,
    edge_fine,
    edge_coarse,
    counts,
    load_sem,
    fine_out,
    coarse_out,
    up_out,
    down_out,
    store_sem,
    u_send,
    u_recv,
    g_own,
    g_recv,
    slope_f,
    fine_t,
    adj_up,
    terms,
    half_recv,
    half_sum,
    peer_recv,
    halo_send_sem,
    halo_recv_sem,
    half_send_sem,
    half_recv_sem,
    peer_send_sem,
    peer_recv_sem,
):
    me = lax.axis_index("patch")
    lower, upper = lax.rem(me + n - 1, n), lax.rem(me + 1, n)
    chips = n // 2
    chip, core = me // 2, lax.rem(me, 2)
    partner = chip * 2 + (1 - core)
    fine_count, width = fine_ref.shape
    coarse_count = coarse_ref.shape[0]
    edge_count = edge_fine.shape[1]
    blocks = counts.shape[1]
    block_len = edge_count // blocks
    own_rows, side_rows = NB_OWN * block_len, NB_SIDE * block_len
    chunk = width // n
    scale = 1.0 / math.sqrt(n * edge_count)
    wire = terms.dtype

    def peer(k):
        return lax.rem(chip + k, chips) * 2 + core

    loads = [
        pltpu.make_async_copy(src, dst, load_sem.at[i])
        for i, (src, dst) in enumerate(
            (
                (counts_hbm, counts),
                (edge_coarse_hbm, edge_coarse),
                (edge_fine_hbm, edge_fine),
                (fine_cot_hbm, fine_cot),
                (down_w_hbm, down_w),
                (coarse_hbm, coarse_ref),
                (coarse_cot_hbm, coarse_cot),
                (fine_hbm, fine_ref),
                (up_w_hbm, up_w),
            )
        )
    ]
    for copy in loads:
        copy.start()
    stores = [
        pltpu.make_async_copy(src, dst, store_sem.at[i])
        for i, (src, dst) in enumerate(
            (
                (fine_out, fine_hbm_out),
                (coarse_out, coarse_hbm_out),
                (up_out, up_hbm_out),
                (down_out, down_hbm_out),
            )
        )
    ]
    barrier = pltpu.get_barrier_semaphore()
    for device in [lower, upper] + [peer(k) for k in range(1, chips)]:
        pl.semaphore_signal(barrier, inc=1, device_id={"patch": device}, device_id_type=MESH)

    for copy in loads[:3]:
        copy.wait()
    spread = lax.broadcasted_iota(jnp.int32, (blocks, edge_count), 1) // block_len
    spread = spread == lax.broadcasted_iota(jnp.int32, (blocks, edge_count), 0)
    spread = jnp.where(spread, 1.0, 0.0).astype(BF16)
    count_rows = mm(counts[...].astype(F32).astype(BF16), spread, NN)
    position = lax.broadcasted_iota(jnp.int32, (1, edge_count), 1) % block_len
    regions = (
        (0, own_rows, me),
        (own_rows, side_rows, lower),
        (own_rows + side_rows, side_rows, upper),
    )

    def selectors(direction, region):
        start, size, owner = region
        lanes = slice(start, start + size)
        valid = position[:, lanes] < count_rows[direction : direction + 1, lanes].astype(jnp.int32)
        coarse = edge_coarse[direction : direction + 1, lanes] - owner * coarse_count
        coarse = jnp.where(valid, coarse, -1)
        fine = edge_fine[direction : direction + 1, lanes] - me * fine_count
        return one_hot(coarse, coarse_count), one_hot(fine, fine_count)

    def down_adjacency(region):
        coarse_sel, fine_sel = selectors(1, region)
        return mm(coarse_sel, fine_sel, NT).astype(BF16)

    def remote(src, dst, send_sem, recv_sem, device):
        return pltpu.make_async_remote_copy(
            src_ref=src,
            dst_ref=dst,
            send_sem=send_sem,
            recv_sem=recv_sem,
            device_id={"patch": device},
            device_id_type=MESH,
        )

    u_copies = [
        remote(
            u_send.at[s], u_recv.at[s], halo_send_sem.at[s], halo_recv_sem.at[s], (lower, upper)[s]
        )
        for s in range(2)
    ]
    adj_lower, adj_upper = down_adjacency(regions[1]), down_adjacency(regions[2])
    loads[3].wait()
    u_send[0] = mm(adj_lower, fine_cot[...], NN).astype(BF16)
    pl.semaphore_wait(barrier, chips + 1)
    u_copies[0].start()
    u_send[1] = mm(adj_upper, fine_cot[...], NN).astype(BF16)
    u_copies[1].start()

    u_sum = mm(down_adjacency(regions[0]), fine_cot[...], NN)
    for copy in loads[4:]:
        copy.wait()
    slope_c = silu_slope(mm(coarse_ref[...], down_w[...], NN))
    fine_t[...] = fine_ref[...].T
    slope_f[...] = silu_slope(mm(fine_ref[...], up_w[...], NN))

    for copy in u_copies:
        copy.wait()
    u_sum = u_sum + u_recv[0].astype(F32) + u_recv[1].astype(F32)
    delta_c = (slope_c * u_sum).astype(BF16)
    coarse_grad = coarse_cot[...].astype(F32) + mm(delta_c, down_w[...], NT)
    coarse_out[...] = coarse_grad
    g_own[...] = coarse_grad.astype(BF16)
    g_copies = [
        remote(
            g_own, g_recv.at[s], halo_send_sem.at[2 + s], halo_recv_sem.at[2 + s], (lower, upper)[s]
        )
        for s in range(2)
    ]
    for copy in g_copies:
        copy.start()
    stores[1].start()

    def half_copy(which):
        return remote(
            terms.at[which, 1 - core],
            half_recv.at[which],
            half_send_sem.at[which],
            half_recv_sem.at[which],
            partner,
        )

    def put_term(which, term):
        term = term.reshape(chips, 2, chunk, width)
        for parity in range(2):
            terms[which, parity] = term[:, parity].astype(wire)
        half_copy(which).start()

    def peer_copy(which, k):
        return remote(
            half_sum.at[which, lax.rem(chip + k, chips)],
            peer_recv.at[which, k - 1],
            peer_send_sem.at[which, k - 1],
            peer_recv_sem.at[which, k - 1],
            peer(k),
        )

    def send_peers(which):
        half_copy(which).wait()
        total = terms[which, core].astype(F32) + half_recv[which].astype(F32)
        half_sum[which] = total.astype(wire)
        for k in range(1, chips):
            peer_copy(which, k).start()

    def finish(which, out_ref):
        total = half_sum[which, chip].astype(F32)
        for k in range(1, chips):
            peer_copy(which, k).wait()
            total = total + peer_recv[which, k - 1].astype(F32)
        out_ref[...] = total * scale

    put_term(0, mm(coarse_ref[...], delta_c, TN))
    for i, region in enumerate(regions):
        coarse_sel, fine_sel = selectors(0, region)
        adj_up[i] = mm(fine_sel, coarse_sel, NT).astype(BF16)
    v_sum = mm(adj_up[0], g_own[...], NN)
    for copy in g_copies:
        copy.wait()
    send_peers(0)
    v_sum = v_sum + mm(adj_up[1], g_recv[1], NN) + mm(adj_up[2], g_recv[0], NN)
    delta_f = (slope_f[...] * v_sum).astype(BF16)
    put_term(1, mm(fine_t[...], delta_f, NN))
    fine_sum = mm(delta_f, up_w[...], NT)
    fine_out[...] = (fine_cot[...].astype(F32) + fine_sum).astype(BF16)
    stores[0].start()
    send_peers(1)
    finish(0, down_out)
    stores[3].start()
    finish(1, up_out)
    stores[2].start()
    for copy in stores:
        copy.wait()


def store_kernel(*refs):
    sources, results, stages = refs[:4], refs[4:8], refs[8:12]
    load_sem, save_sem = refs[12:]
    loads = [
        pltpu.make_async_copy(src, stage, load_sem.at[i])
        for i, (src, stage) in enumerate(zip(sources, stages))
    ]
    saves = [
        pltpu.make_async_copy(stage, dst, save_sem.at[i])
        for i, (stage, dst) in enumerate(zip(stages, results))
    ]
    for copy in loads:
        copy.start()
    for load, save in zip(loads[::-1], saves[::-1]):
        load.wait()
        save.start()
    for copy in saves:
        copy.wait()


def on_device(
    fine_latents,
    coarse_latents,
    up_weight,
    down_weight,
    fine_cotangent,
    coarse_cotangent,
    edge_fine,
    edge_coarse,
    block_counts,
):
    n = lax.axis_size("patch")
    fine_count, width = fine_latents.shape
    coarse_count = coarse_latents.shape[0]
    chunk, chips = width // n, n // 2
    wire = BF16 if chunk % 16 == 0 else F32
    hbm = pl.BlockSpec(memory_space=pltpu.HBM)
    dma = pltpu.SemaphoreType.DMA
    arguments = (
        fine_latents,
        coarse_latents,
        up_weight,
        down_weight,
        fine_cotangent,
        coarse_cotangent,
        edge_fine,
        edge_coarse,
        block_counts,
    )
    out_shape = (
        jax.ShapeDtypeStruct((fine_count, width), BF16),
        jax.ShapeDtypeStruct((coarse_count, width), F32),
        jax.ShapeDtypeStruct((chunk, width), F32),
        jax.ShapeDtypeStruct((chunk, width), F32),
    )
    results = pl.pallas_call(
        functools.partial(kernel, n),
        out_shape=out_shape,
        in_specs=[hbm] * 9,
        out_specs=[hbm] * 4,
        scratch_shapes=[pltpu.VMEM(value.shape, value.dtype) for value in arguments]
        + [
            dma((9,)),
        ]
        + [pltpu.VMEM(value.shape, value.dtype) for value in out_shape]
        + [
            dma((4,)),
            pltpu.VMEM((2, coarse_count, width), BF16),
            pltpu.VMEM((2, coarse_count, width), BF16),
            pltpu.VMEM((coarse_count, width), BF16),
            pltpu.VMEM((2, coarse_count, width), BF16),
            pltpu.VMEM((fine_count, width), F32),
            pltpu.VMEM((width, fine_count), BF16),
            pltpu.VMEM((3, fine_count, coarse_count), BF16),
            pltpu.VMEM((2, 2, chips, chunk, width), wire),
            pltpu.VMEM((2, chips, chunk, width), wire),
            pltpu.VMEM((2, chips, chunk, width), wire),
            pltpu.VMEM((2, chips - 1, chunk, width), wire),
            dma((4,)),
            dma((4,)),
            dma((2,)),
            dma((2,)),
            dma((2, chips - 1)),
            dma((2, chips - 1)),
        ],
        compiler_params=pltpu.CompilerParams(
            collective_id=0, has_side_effects=True, vmem_limit_bytes=VMEM_LIMIT
        ),
        cost_estimate=pl.CostEstimate(
            flops=4 * 10**9, bytes_accessed=4 * 10**6, transcendentals=4 * 10**5
        ),
    )(*arguments)
    return pl.pallas_call(
        store_kernel,
        out_shape=out_shape,
        in_specs=[hbm] * 4,
        out_specs=[hbm] * 4,
        scratch_shapes=[pltpu.VMEM(value.shape, value.dtype) for value in out_shape]
        + [dma((4,)), dma((4,))],
        compiler_params=pltpu.CompilerParams(vmem_limit_bytes=VMEM_LIMIT),
    )(*results)


def solution(mesh):
    nodes = P(("groups", "patch"), None)
    edges = P(None, "patch")
    return jax.shard_map(
        on_device,
        mesh=mesh,
        in_specs=(nodes, nodes, P(), P(), nodes, nodes, edges, edges, edges),
        out_specs=(nodes, nodes, nodes, nodes),
        check_vma=False,
    )
```
